512 devices in a mesh: dp: 32 (over z, core), tensor: 16 (over y, x).
Axes of the slice: x: 4, y: 4, z: 16, core: 2. Of those that a mesh axis runs over, the one named last changes fastest.
Arguments:
- hidden: bfloat16 [4096, 18432], P('dp', 'tensor'), may hold values from -66 to 66
- grad_out: bfloat16 [4096, 4608], P('dp'), may hold values from -192 to 192
- seg_ids: int32 [4096], replicated, may hold values from 0 to 7, as said below
- seg_counts: int32 [256], P('dp'), may hold values from 1 to 31, as said below
- added_noise: bfloat16 [4608, 18432], P('dp', 'tensor'), may hold values from -6 to 6
Outputs:
- weight_grad: bfloat16 [4608, 18432], P('dp', 'tensor')
- example_norms: float32 [256], P('dp')
The draws below stay inside these ranges and needn't reach their ends.
Inputs may be any that keep to these rules, and one draw needn't show every extreme that they name: `seg_ids`: within each sequence the ids never fall and every one of the 8 ids occurs. seg_counts[j * 8 + i] is the number of tokens of sequence j whose id is i; the counts of a sequence sum to 128.
All inputs are finite; a program needn't handle non-finite values.
Results may differ from the reference program's by a relative error of at most 0.012.
Values may be sent and summed in bfloat16 or wider, within the bound.
No kernel may reach another device: no remote copies, remote signals or barrier semaphores. Data moves between devices by JAX's collectives and lax.ppermute only.
A program may use at most 64 MiB of HBM per device.

```python
import math
import jax
import jax.numpy as jnp
from jax import lax

D = 4608
FFW = 18432
SEQ = 128
NSEG = 8
TOKENS = 4096
EXAMPLES = 256


def segment_lengths(key):
    groups = TOKENS // SEQ
    width = SEQ // NSEG
    key_shift, key_order = jax.random.split(key)
    shifts = jax.random.randint(key_shift, (groups, NSEG // 2), 1 - width, width)
    shifts = shifts.at[:, 0].set(width - 1)
    lengths = jnp.concatenate([width + shifts, width - shifts], axis=1)
    order_keys = jax.random.split(key_order, groups)
    permuted = jax.vmap(lambda item_key: jax.random.permutation(item_key, NSEG))(order_keys)
    return jnp.take_along_axis(lengths, permuted, axis=1).astype(jnp.int32)


def token_segments(lengths):
    bounds = jnp.cumsum(lengths, axis=1)
    positions = jnp.arange(SEQ, dtype=jnp.int32)
    return jnp.sum((positions[None, :, None] >= bounds[:, None, :NSEG - 1]).astype(jnp.int32), axis=2).astype(jnp.int32)


def draw_seg_counts(key, part):
    lengths = segment_lengths(key)
    return lengths.reshape(EXAMPLES).astype(jnp.int32)


def draw_seg_ids(key, part):
    segments = token_segments(segment_lengths(key))
    return segments.reshape(TOKENS).astype(jnp.int32)


def scaled_field(key, rows, columns, spread, entries):
    key_rows, key_columns = jax.random.split(key)
    reach = math.log(spread)
    row_scale = jnp.exp(jax.random.uniform(key_rows, (rows, 1), jnp.float32, -reach, reach))
    column_scale = jnp.exp(jax.random.uniform(key_columns, (1, columns), jnp.float32, -reach, reach))
    return entries * row_scale * column_scale


def draw_hidden(key, part):
    key = jax.random.fold_in(key, 5)
    key_main = jax.random.fold_in(key, 0)
    key_scale = jax.random.fold_in(key, 2)
    entries = jnp.clip(jax.random.normal(key_main, (TOKENS, FFW), jnp.float32), -6.0, 6.0)
    spread = 3.1622777
    return scaled_field(key_scale, TOKENS, FFW, spread, entries).astype(jnp.bfloat16)


def draw_grad_out(key, part):
    segments = token_segments(segment_lengths(key))
    key = jax.random.fold_in(key, 6)
    key_main = jax.random.fold_in(key, 0)
    key_scale = jax.random.fold_in(key, 2)
    key_example = jax.random.fold_in(key, 3)
    groups = TOKENS // SEQ
    example_scale = jnp.exp(jax.random.uniform(key_example, (groups, NSEG), jnp.float32, -1.0986123, 1.0986123))
    tok_scale = jnp.take_along_axis(example_scale, segments, axis=1).reshape(TOKENS, 1)
    entries = jnp.clip(jax.random.normal(key_main, (TOKENS, D), jnp.float32), -6.0, 6.0)
    spread = 3.1622777
    field = scaled_field(key_scale, TOKENS, D, spread, entries) * tok_scale
    return field.astype(jnp.bfloat16)


def levels(own_key, extent, shards, least, high):
    gain = 1.0
    for axis_at, shards_of in shards:
        draws = jax.random.uniform(jax.random.fold_in(jax.random.fold_in(own_key, 6), axis_at), (shards_of,), jnp.float32, least / len(shards), high / len(shards))
        gain = gain * jnp.repeat(jnp.exp(draws), extent[axis_at] // shards_of).reshape((-1,) + (1,) * (len(extent) - 1 - axis_at))
    return gain


def centred(stream_key, dims, scale, most, pieces=(), kind=jnp.bfloat16):
    factor_of = levels(stream_key, dims, pieces, -0.22, 0.18) if pieces else 1.0
    drawn = jax.random.normal(stream_key, dims, jnp.float32) * scale * factor_of
    return jnp.minimum(jnp.maximum(drawn, -most), most).astype(kind)


def setup_inputs(seed: int = 0) -> dict:
    splits = jax.random.split(jax.random.key(seed), 6)
    hidden = draw_hidden(jax.random.fold_in(splits[5], 71), 0)
    grad_out = draw_grad_out(jax.random.fold_in(splits[5], 71), 0)
    seg_ids = draw_seg_ids(jax.random.fold_in(splits[5], 71), 0)
    seg_counts = draw_seg_counts(jax.random.fold_in(splits[5], 71), 0)
    added_noise = centred(splits[4], (D, FFW), 1.0, 6.0, ((0, 32), (1, 16)))
    return {"hidden": hidden, "grad_out": grad_out, "seg_ids": seg_ids, "seg_counts": seg_counts, "added_noise": added_noise}


EPSILON = 1e-06
CLIP_FRACTION = 4.2

def clip_bound():
    return CLIP_FRACTION * (FFW * D * NSEG / SEQ) ** 0.5

def group_squares(item):
    hidden_group, scaled_group, segment_group = item
    hidden_wide = hidden_group.astype(jnp.float32)
    scaled_wide = scaled_group.astype(jnp.float32)
    gram_hidden = jnp.dot(hidden_wide, hidden_wide.T, precision=lax.Precision.HIGHEST)
    gram_scaled = jnp.dot(scaled_wide, scaled_wide.T, precision=lax.Precision.HIGHEST)
    member = (segment_group[:, None] == jnp.arange(NSEG, dtype=jnp.int32)[None, :]).astype(jnp.float32)
    products = gram_hidden * gram_scaled
    return lax.optimization_barrier(jnp.sum(member * jnp.dot(products, member, precision=lax.Precision.HIGHEST), axis=0))

def reference(hidden, grad_out, seg_ids, seg_counts, added_noise):
    groups = TOKENS // SEQ
    segments = seg_ids.reshape(groups, SEQ).astype(jnp.int32)
    counts = seg_counts.reshape(groups, NSEG).astype(jnp.float32)
    tok_count = jnp.take_along_axis(counts, segments, axis=1)
    scaled = (grad_out.reshape(groups, SEQ, D).astype(jnp.float32) / tok_count[:, :, None]).astype(jnp.bfloat16)
    squares = lax.map(group_squares, (hidden.reshape(groups, SEQ, FFW), scaled, segments))
    norms = jnp.sqrt(squares + EPSILON)
    factors = jnp.minimum(1.0, clip_bound() / norms)
    tok_factor = jnp.take_along_axis(factors, segments, axis=1)
    weighted = (scaled.astype(jnp.float32) * tok_factor[:, :, None]).astype(jnp.bfloat16).reshape(TOKENS, D)
    summed = lax.dot_general(weighted.astype(jnp.float32), hidden.astype(jnp.float32), (((0,), (0,)), ((), ())), precision=lax.Precision.HIGHEST)
    weight_grad = (summed + added_noise.astype(jnp.float32)).astype(jnp.bfloat16)
    return (weight_grad, norms.reshape(EXAMPLES))
```

```python
import jax
import jax.numpy as jnp
from jax import lax
from jax.experimental import pallas as pl
from jax.experimental.pallas import tpu as pltpu
from jax.sharding import PartitionSpec as P

D = 4608
FFW = 18432
SEQ = 128
NSEG = 8
PLANES = 16
ROW = 4
ROWS = 144

EPSILON = 1e-06
CLIP_FRACTION = 4.2


def clip_bound():
    return CLIP_FRACTION * (FFW * D * NSEG / SEQ) ** 0.5


def mix(value, stride):
    return [
        lax.ppermute(value, "tensor", [(i, i ^ (k * stride)) for i in range(ROW * ROW)])
        for k in range(1, ROW)
    ]


def plane_sum(value):
    for stride in (1, ROW):
        one, two, three = mix(value, stride)
        value = (value + one) + (two + three)
    return value


def plane_gather(value):
    for stride in (1, ROW):
        value = jnp.concatenate([value] + mix(value, stride), axis=0)
    return value


def shift_perm(cross):
    perm = []
    for plane in range(PLANES):
        for core in range(2):
            for j in range(ROW * ROW):
                to = ((plane + j) % PLANES) * 2 + (1 - core if cross else core)
                perm.append(((plane * 2 + core) * 16 + j, to * 16 + j))
    return perm


def product_kernel(place, w_ref, h_ref, noise_ref, out_ref, acc_ref):
    step = pl.program_id(0)

    @pl.when(step == 0)
    def _():
        acc_ref[...] = jnp.zeros_like(acc_ref)

    acc_ref[...] += jnp.dot(w_ref[0], h_ref[0], preferred_element_type=jnp.float32)

    @pl.when(step == pl.num_programs(0) - 1)
    def _():
        out_ref[...] = (acc_ref[...] + noise_ref[...].astype(jnp.float32)).astype(jnp.bfloat16)


def product(place, w_all, h_all, noise):
    columns = h_all.shape[-1]
    return pl.pallas_call(
        product_kernel,
        grid_spec=pltpu.PrefetchScalarGridSpec(
            num_scalar_prefetch=1,
            grid=(PLANES,),
            in_specs=[
                pl.BlockSpec((1, ROWS, 256), lambda s, p: (((p[0] + PLANES - s) % PLANES) ^ p[1], 0, 0)),
                pl.BlockSpec((1, 256, columns), lambda s, p: (s, 0, 0)),
                pl.BlockSpec((ROWS, columns), lambda s, p: (0, 0)),
            ],
            out_specs=pl.BlockSpec((ROWS, columns), lambda s, p: (0, 0)),
            scratch_shapes=[pltpu.VMEM((ROWS, columns), jnp.float32)],
        ),
        out_shape=jax.ShapeDtypeStruct((ROWS, columns), jnp.bfloat16),
        compiler_params=pltpu.CompilerParams(vmem_limit_bytes=24 * 1024 * 1024),
        cost_estimate=pl.CostEstimate(
            flops=2 * 4096 * ROWS * columns, bytes_accessed=2 * 4096 * (ROWS + columns), transcendentals=0
        ),
    )(place, w_all, h_all, noise)


def per_device(hidden, grad_out, seg_ids, seg_counts, added_noise):
    dp = lax.axis_index("dp")
    j = lax.axis_index("tensor")
    plane, core = dp // 2, dp % 2
    h_all = lax.all_gather(hidden, "dp", axis=0, tiled=True)

    own = lax.dynamic_slice_in_dim(seg_ids, dp * SEQ, SEQ)
    member = own[:, None] == jnp.arange(NSEG, dtype=jnp.int32)[None, :]
    same = own[:, None] == own[None, :]

    def per_token(values):
        return jnp.sum(jnp.where(member, values[None, :], 0.0), axis=1)

    tok_count = per_token(seg_counts.astype(jnp.float32))
    scaled = (grad_out.astype(jnp.float32) / tok_count[:, None]).astype(jnp.bfloat16)
    contract = (((1,), (1,)), ((), ()))
    gram_scaled = lax.dot_general(scaled, scaled, contract, preferred_element_type=jnp.float32)
    gram_hidden = lax.dot_general(hidden, hidden, contract, preferred_element_type=jnp.float32)
    rows = jnp.sum(jnp.where(same, gram_hidden * gram_scaled, 0.0), axis=1)
    partial_sq = jnp.sum(jnp.where(member, rows[:, None], 0.0), axis=0)
    own_norm = jnp.sqrt(plane_sum(partial_sq) + EPSILON)
    tok_factor = per_token(jnp.minimum(1.0, clip_bound() / own_norm))

    target = (plane + j) % PLANES
    piece = lax.dynamic_slice_in_dim(scaled, target * (2 * ROWS), 2 * ROWS, 1)
    piece = (piece.astype(jnp.float32) * tok_factor[:, None]).astype(jnp.bfloat16).T
    first = core == 0
    keep = lax.ppermute(jnp.where(first, piece[:ROWS], piece[ROWS:]), ("dp", "tensor"), shift_perm(False))
    swap = lax.ppermute(jnp.where(first, piece[ROWS:], piece[:ROWS]), ("dp", "tensor"), shift_perm(True))
    block = jnp.concatenate([jnp.where(first, keep, swap), jnp.where(first, swap, keep)], axis=1)
    w_all = plane_gather(block[None])

    place = jnp.stack([plane, j]).astype(jnp.int32)
    weight_grad = product(place, w_all, h_all.reshape(PLANES, 2 * SEQ, -1), added_noise)
    return (weight_grad, own_norm)


def solution(mesh):
    placed = (P("dp", "tensor"), P("dp", None), P(), P("dp"), P("dp", "tensor"))
    return jax.shard_map(
        per_device,
        mesh=mesh,
        in_specs=placed,
        out_specs=(P("dp", "tensor"), P("dp")),
        check_vma=False,
    )
```

```python
import jax
import jax.numpy as jnp
from jax import lax
from jax.experimental import pallas as pl
from jax.experimental.pallas import tpu as pltpu
from jax.sharding import Mesh
from jax.sharding import PartitionSpec as P

D = 4608
FFW = 18432
SEQ = 128
NSEG = 8
PLANES = 16
ROW = 4
ROWS = 144

EPSILON = 1e-06
CLIP_FRACTION = 4.2


def clip_bound():
    return CLIP_FRACTION * (FFW * D * NSEG / SEQ) ** 0.5


def along_y(value, distance):
    return lax.ppermute(value, "y", [(i, i ^ distance) for i in range(ROW)])


def fan_out(value, extra, cross):
    perm = []
    for plane in range(PLANES):
        for core in range(2):
            for j in range(ROW * ROW):
                to = ((plane + j + extra) % PLANES) * 2 + (1 - core if cross else core)
                perm.append(((plane * 2 + core) * 16 + j, to * 16 + j))
    return lax.ppermute(value, ("dp", "y", "x"), perm)


def squares_kernel(place, seg_ref, count_ref, hidden_ref, grad_ref, out_ref, count_column_ref, gram_ref):
    step = pl.program_id(0)
    seg = seg_ref[pl.ds(place[0], 1), :]
    row = lax.broadcasted_iota(jnp.int32, (SEQ, SEQ), 0)
    column = lax.broadcasted_iota(jnp.int32, (SEQ, SEQ), 1)

    @pl.when(step == 0)
    def _():
        count = jnp.zeros((1, SEQ), jnp.float32)
        for i in range(NSEG):
            count = jnp.where(seg == i, count_ref[i].astype(jnp.float32), count)
        count_column_ref[...] = jnp.sum(jnp.where(row == column, count, 0.0), axis=1, keepdims=True)
        gram_ref[...] = jnp.zeros_like(gram_ref)

    contract = (((1,), (1,)), ((), ()))
    scaled = (grad_ref[...].astype(jnp.float32) / count_column_ref[...]).astype(jnp.bfloat16)
    gram_ref[...] += lax.dot_general(scaled, scaled, contract, preferred_element_type=jnp.float32)

    @pl.when(step == pl.num_programs(0) - 1)
    def _():
        gram_hidden = lax.dot_general(
            hidden_ref[...], hidden_ref[...], contract, preferred_element_type=jnp.float32
        )
        seg_wide = seg.astype(jnp.float32)
        seg_column = jnp.sum(jnp.where(row == column, seg_wide, 0.0), axis=1, keepdims=True)
        products = jnp.where(seg_column == seg_wide, gram_hidden * gram_ref[...], 0.0)
        columns = jnp.sum(products, axis=0, keepdims=True)
        example = lax.broadcasted_iota(jnp.int32, (NSEG, SEQ), 0)
        total = jnp.sum(jnp.where(example == seg, columns, 0.0), axis=1, keepdims=True)
        out_ref[...] = jnp.broadcast_to(total, (NSEG, SEQ))


def partial_squares(dp, seg_rows, counts, hidden, grad_out):
    width = 1536
    return pl.pallas_call(
        squares_kernel,
        grid_spec=pltpu.PrefetchScalarGridSpec(
            num_scalar_prefetch=1,
            grid=(D // width,),
            in_specs=[
                pl.BlockSpec(seg_rows.shape, lambda k, p: (0, 0)),
                pl.BlockSpec(memory_space=pltpu.SMEM),
                pl.BlockSpec(hidden.shape, lambda k, p: (0, 0)),
                pl.BlockSpec((SEQ, width), lambda k, p: (0, k)),
            ],
            out_specs=pl.BlockSpec((NSEG, SEQ), lambda k, p: (0, 0)),
            scratch_shapes=[pltpu.VMEM((SEQ, 1), jnp.float32), pltpu.VMEM((SEQ, SEQ), jnp.float32)],
        ),
        out_shape=jax.ShapeDtypeStruct((NSEG, SEQ), jnp.float32),
        compiler_params=pltpu.CompilerParams(vmem_limit_bytes=56 * 1024 * 1024),
    )(dp[None], seg_rows, counts, hidden, grad_out)


def order_kernel(place, *refs):
    quarters, out_ref = refs[:ROW], refs[ROW]
    for i in range(2 * PLANES):
        for k in range(ROW):

            @pl.when(place[0, i] == k)
            def _(i=i, k=k):
                out_ref[:, i * SEQ : (i + 1) * SEQ] = quarters[k][place[1, i]]


def in_order(place, quarters):
    vmem = pl.BlockSpec(memory_space=pltpu.VMEM)
    return pl.pallas_call(
        order_kernel,
        in_specs=[pl.BlockSpec(memory_space=pltpu.SMEM)] + [vmem] * ROW,
        out_specs=vmem,
        out_shape=jax.ShapeDtypeStruct((ROWS, 2 * PLANES * SEQ), jnp.bfloat16),
        compiler_params=pltpu.CompilerParams(vmem_limit_bytes=24 * 1024 * 1024),
    )(place, *quarters)


def per_device(hidden, grad_out, seg_ids, seg_counts, added_noise):
    dp = lax.axis_index("dp")
    x, y = lax.axis_index("x"), lax.axis_index("y")
    plane, core, j = dp // 2, dp % 2, y * ROW + x
    h_all = lax.all_gather(hidden, "dp", axis=0, tiled=True)

    seg_rows = seg_ids.reshape(-1, SEQ)
    member = lax.dynamic_slice_in_dim(seg_rows, dp, 1, 0) == jnp.arange(NSEG, dtype=jnp.int32)[:, None]

    def per_token(values):
        return jnp.sum(jnp.where(member, values[:, None], 0.0), axis=0, keepdims=True)

    counts = per_token(seg_counts.astype(jnp.float32))
    squares = partial_squares(dp, seg_rows, seg_counts, hidden, grad_out)

    def piece(target, of_core):
        start = (target % PLANES * 2 + of_core) * ROWS
        block = lax.dynamic_slice_in_dim(grad_out, start, ROWS, 1).T
        return (block.astype(jnp.float32) / counts).astype(jnp.bfloat16)

    keep, swap = piece(plane + j, core), piece(plane + j + 8, 1 - core)
    keep, swap, squares = lax.optimization_barrier((keep, swap, squares))
    norms = jnp.sqrt(lax.psum(lax.psum(squares, "x"), "y")[:, 0] + EPSILON)
    factor = per_token(jnp.minimum(1.0, clip_bound() / norms))

    def weighted(scaled):
        return (scaled.astype(jnp.float32) * factor).astype(jnp.bfloat16)

    keep, swap = fan_out(weighted(keep), 0, False), fan_out(weighted(swap), 8, True)
    row = lax.all_gather(jnp.stack([keep, swap]), "x", axis=0, tiled=True)
    quarters = [row] + [along_y(row, k) for k in range(1, ROW)]

    sequence = jnp.arange(2 * PLANES)
    other = (sequence % 2 != core).astype(jnp.int32)
    came = (plane - sequence // 2 + 2 * PLANES - 8 * other) % PLANES
    place = jnp.stack([(came // ROW) ^ y, (came % ROW) * 2 + other]).astype(jnp.int32)
    w_rows = in_order(place, quarters)
    summed = jnp.dot(w_rows, h_all, preferred_element_type=jnp.float32)
    weight_grad = (summed + added_noise.astype(jnp.float32)).astype(jnp.bfloat16)
    return (weight_grad, norms)


def solution(mesh):
    split = Mesh(mesh.devices.reshape(-1, ROW, ROW), ("dp", "y", "x"))
    tensor = ("y", "x")
    placed = (P("dp", tensor), P("dp", None), P(), P("dp"), P("dp", tensor))
    return jax.shard_map(
        per_device,
        mesh=split,
        in_specs=placed,
        out_specs=(P("dp", tensor), P("dp")),
        check_vma=False,
    )
```

```python
import functools

import jax
import jax.numpy as jnp
from jax import lax
from jax.experimental import pallas as pl
from jax.experimental.pallas import tpu as pltpu
from jax.sharding import Mesh
from jax.sharding import PartitionSpec as P

D = 4608
FFW = 18432
SEQ = 128
NSEG = 8
PLANES = 16
PAIRS = PLANES // 2
ROW = 4
ROWS = 144

EPSILON = 1e-06
CLIP_FRACTION = 4.2


def clip_bound():
    return CLIP_FRACTION * (FFW * D * NSEG / SEQ) ** 0.5


def along_y(value, distance):
    return lax.ppermute(value, "y", [(i, i ^ distance) for i in range(ROW)])


def fan_out(value, extra, cross):
    perm = []
    for plane in range(PLANES):
        for core in range(2):
            for j in range(ROW * ROW):
                to = ((plane + 2 * (j % PAIRS + extra)) % PLANES) * 2 + (1 - core if cross else core)
                perm.append(((plane * 2 + core) * 16 + j, to * 16 + j))
    return lax.ppermute(value, ("pair", "parity", "core", "y", "x"), perm)


def to_neighbour(value):
    perm = [(plane * 2 + core, (plane + 1 - 2 * core) % PLANES * 2 + core) for plane in range(PLANES) for core in range(2)]
    return lax.ppermute(value, ("pair", "parity", "core"), perm)


def squares_kernel(place, seg_ref, count_ref, hidden_ref, grad_ref, out_ref, keep_ref, swap_ref, turned_ref):
    seg = seg_ref[pl.ds(place[0], 1), :]
    row = lax.broadcasted_iota(jnp.int32, (SEQ, SEQ), 0)
    column = lax.broadcasted_iota(jnp.int32, (SEQ, SEQ), 1)
    count = jnp.zeros((1, SEQ), jnp.float32)
    for i in range(NSEG):
        count = jnp.where(seg == i, count_ref[i].astype(jnp.float32), count)
    count_column = jnp.sum(jnp.where(row == column, count, 0.0), axis=1, keepdims=True)

    def scaled(block):
        return (block.astype(jnp.float32) / count_column).astype(jnp.bfloat16)

    contract = (((1,), (1,)), ((), ()))
    gram_hidden = lax.dot_general(
        hidden_ref[...], hidden_ref[...], contract, preferred_element_type=jnp.float32
    )
    gram_scaled = jnp.zeros((SEQ, SEQ), jnp.float32)
    width = 512
    for k in range(D // width):
        block = scaled(grad_ref[:, k * width : (k + 1) * width])
        gram_scaled += lax.dot_general(block, block, contract, preferred_element_type=jnp.float32)
    seg_wide = seg.astype(jnp.float32)
    seg_column = jnp.sum(jnp.where(row == column, seg_wide, 0.0), axis=1, keepdims=True)
    products = jnp.where(seg_column == seg_wide, gram_hidden * gram_scaled, 0.0)
    columns = jnp.sum(products, axis=0, keepdims=True)
    example = lax.broadcasted_iota(jnp.int32, (NSEG, SEQ), 0)
    total = jnp.sum(jnp.where(example == seg, columns, 0.0), axis=1, keepdims=True)
    of_token = jnp.sum(jnp.where(example == seg, total, 0.0), axis=0, keepdims=True)
    out_ref[:NSEG, :] = jnp.broadcast_to(total, (NSEG, SEQ))
    out_ref[NSEG:, :] = jnp.broadcast_to(of_token, (NSEG, SEQ))

    window = turned_ref.shape[0]
    for n, piece_ref in enumerate((keep_ref, swap_ref)):
        start = place[1 + n]
        at = pl.multiple_of(jnp.minimum(start // SEQ * SEQ, D - window), SEQ)
        turned_ref[...] = scaled(grad_ref[:, pl.ds(at, window)]).astype(jnp.float32).T
        inside = pl.multiple_of(start - at, 16)
        piece_ref[...] = turned_ref[pl.ds(inside, ROWS), :].astype(jnp.bfloat16)


def partial_squares(place, seg_rows, counts, hidden, grad_out):
    vmem, smem = pl.BlockSpec(memory_space=pltpu.VMEM), pl.BlockSpec(memory_space=pltpu.SMEM)
    piece = jax.ShapeDtypeStruct((ROWS, SEQ), jnp.bfloat16)
    return pl.pallas_call(
        squares_kernel,
        in_specs=[smem, vmem, smem, vmem, vmem],
        out_specs=[vmem] * 3,
        out_shape=[jax.ShapeDtypeStruct((2 * NSEG, SEQ), jnp.float32), piece, piece],
        scratch_shapes=[pltpu.VMEM((3 * SEQ, SEQ), jnp.float32)],
        compiler_params=pltpu.CompilerParams(vmem_limit_bytes=56 * 1024 * 1024),
    )(place, seg_rows, counts, hidden, grad_out)


def product_kernel(own, place, *refs):
    quarters, h_ref, rest = refs[:ROW], refs[ROW], refs[ROW + 1 :]
    out_ref, w_ref = rest[-2], rest[-1]
    for i in range(PLANES):
        for k in range(ROW):

            @pl.when(place[0, i] == k)
            def _(i=i, k=k):
                w_ref[:, i * SEQ : (i + 1) * SEQ] = quarters[k][place[1, i]]

    summed = jnp.dot(w_ref[...], h_ref[...], preferred_element_type=jnp.float32)
    if own:
        summed += rest[0][...].astype(jnp.float32)
    out_ref[...] = summed.astype(out_ref.dtype)


def product(place, quarters, h_all, noise=None):
    own = noise is not None
    tokens, columns = h_all.shape
    vmem = pl.BlockSpec(memory_space=pltpu.VMEM)
    return pl.pallas_call(
        functools.partial(product_kernel, own),
        in_specs=[pl.BlockSpec(memory_space=pltpu.SMEM)] + [vmem] * (ROW + 1 + own),
        out_specs=vmem,
        out_shape=jax.ShapeDtypeStruct((ROWS, columns), jnp.float32 if own else jnp.bfloat16),
        scratch_shapes=[pltpu.VMEM((ROWS, tokens), jnp.bfloat16)],
        compiler_params=pltpu.CompilerParams(vmem_limit_bytes=24 * 1024 * 1024),
        cost_estimate=pl.CostEstimate(
            flops=2 * tokens * ROWS * columns, bytes_accessed=2 * tokens * (ROWS + columns), transcendentals=0
        ),
    )(place, *quarters, h_all, *([noise] if own else []))


def per_device(hidden, grad_out, seg_ids, seg_counts, added_noise):
    pair, parity, core = lax.axis_index("pair"), lax.axis_index("parity"), lax.axis_index("core")
    x, y = lax.axis_index("x"), lax.axis_index("y")
    plane, j = pair * 2 + parity, y * ROW + x
    dp = plane * 2 + core
    h_all = lax.all_gather(hidden, ("pair", "core"), axis=0, tiled=True)

    seg_rows = seg_ids.reshape(-1, SEQ)

    def start(to_plane, of_core):
        shift = jnp.where(y < 2, 0, 1 - 2 * of_core)
        return ((to_plane + shift + PLANES) % PLANES * 2 + of_core) * ROWS

    ahead = plane + 2 * (j % PAIRS)
    here = jnp.stack([dp, start(ahead, core), start(ahead + 8, 1 - core)]).astype(jnp.int32)
    squares, keep, swap = partial_squares(here, seg_rows, seg_counts, hidden, grad_out)
    squares = lax.psum(lax.psum(squares, "x"), "y")
    norms = jnp.sqrt(squares[:NSEG, 0] + EPSILON)
    factor = jnp.minimum(1.0, clip_bound() / jnp.sqrt(squares[NSEG : NSEG + 1] + EPSILON))

    def weighted(scaled):
        return (scaled.astype(jnp.float32) * factor).astype(jnp.bfloat16)

    keep, swap = fan_out(weighted(keep), 0, False), fan_out(weighted(swap), 4, True)
    row = lax.all_gather(jnp.stack([keep, swap]), "x", axis=0, tiled=True)
    one, two, three = [along_y(row, k) for k in range(1, ROW)]
    h_all, three = lax.optimization_barrier((h_all, three))
    quarters = [row, one, two, three]

    sequence = jnp.arange(PLANES)
    other = (sequence % 2 != core).astype(jnp.int32)
    came = (pair - sequence // 2 + 2 * PAIRS - 4 * other) % PAIRS
    inside = came % ROW * 2 + other

    def place(block):
        return jnp.stack([(2 * block + came // ROW) ^ y, inside]).astype(jnp.int32)

    handed = to_neighbour(product(place(1), quarters, h_all))
    summed = product(place(0), quarters, h_all, added_noise)
    weight_grad = (summed + handed.astype(jnp.float32)).astype(jnp.bfloat16)
    return (weight_grad, norms)


def solution(mesh):
    split = Mesh(mesh.devices.reshape(PAIRS, 2, 2, ROW, ROW), ("pair", "parity", "core", "y", "x"))
    dp, tensor = ("pair", "parity", "core"), ("y", "x")
    placed = (P(dp, tensor), P(dp, None), P(), P(dp), P(dp, tensor))
    return jax.shard_map(
        per_device,
        mesh=split,
        in_specs=placed,
        out_specs=(P(dp, tensor), P(dp)),
        check_vma=False,
    )
```

```python
import jax
import jax.numpy as jnp
from jax import lax
from jax.experimental import pallas as pl
from jax.experimental.pallas import tpu as pltpu
from jax.sharding import Mesh
from jax.sharding import PartitionSpec as P

D = 4608
FFW = 18432
SEQ = 128
NSEG = 8
PLANES = 16
PAIRS = PLANES // 2
ROW = 4
ROWS = 144

EPSILON = 1e-06
CLIP_FRACTION = 4.2


def clip_bound():
    return CLIP_FRACTION * (FFW * D * NSEG / SEQ) ** 0.5


def along_y(value, distance):
    return lax.ppermute(value, "y", [(i, i ^ distance) for i in range(ROW)])


def fan_out(value, extra, cross):
    perm = []
    for plane in range(PLANES):
        for core in range(2):
            for j in range(ROW * ROW):
                to = ((plane + 2 * (j % PAIRS + extra)) % PLANES) * 2 + (1 - core if cross else core)
                perm.append(((plane * 2 + core) * 16 + j, to * 16 + j))
    return lax.ppermute(value, ("pair", "parity", "core", "y", "x"), perm)


def to_neighbour(value):
    perm = [(plane * 2 + core, (plane + 1 - 2 * core) % PLANES * 2 + core) for plane in range(PLANES) for core in range(2)]
    return lax.ppermute(value, ("pair", "parity", "core"), perm)


def squares_kernel(place, seg_ref, count_ref, hidden_ref, grad_ref, out_ref, keep_ref, swap_ref, turned_ref):
    seg = seg_ref[pl.ds(place[0], 1), :]
    row = lax.broadcasted_iota(jnp.int32, (SEQ, SEQ), 0)
    column = lax.broadcasted_iota(jnp.int32, (SEQ, SEQ), 1)
    count = jnp.zeros((1, SEQ), jnp.float32)
    for i in range(NSEG):
        count = jnp.where(seg == i, count_ref[i].astype(jnp.float32), count)
    count_column = jnp.sum(jnp.where(row == column, count, 0.0), axis=1, keepdims=True)

    def scaled(block):
        return (block.astype(jnp.float32) / count_column).astype(jnp.bfloat16)

    contract = (((1,), (1,)), ((), ()))
    gram_hidden = lax.dot_general(
        hidden_ref[...], hidden_ref[...], contract, preferred_element_type=jnp.float32
    )
    gram_scaled = jnp.zeros((SEQ, SEQ), jnp.float32)
    width = 512
    for k in range(D // width):
        block = scaled(grad_ref[:, k * width : (k + 1) * width])
        gram_scaled += lax.dot_general(block, block, contract, preferred_element_type=jnp.float32)
    seg_wide = seg.astype(jnp.float32)
    seg_column = jnp.sum(jnp.where(row == column, seg_wide, 0.0), axis=1, keepdims=True)
    products = jnp.where(seg_column == seg_wide, gram_hidden * gram_scaled, 0.0)
    columns = jnp.sum(products, axis=0, keepdims=True)
    example = lax.broadcasted_iota(jnp.int32, (NSEG, SEQ), 0)
    total = jnp.sum(jnp.where(example == seg, columns, 0.0), axis=1, keepdims=True)
    of_token = jnp.sum(jnp.where(example == seg, total, 0.0), axis=0, keepdims=True)
    out_ref[:NSEG, :] = jnp.broadcast_to(total, (NSEG, SEQ))
    out_ref[NSEG:, :] = jnp.broadcast_to(of_token, (NSEG, SEQ))

    window = turned_ref.shape[0]
    for n, piece_ref in enumerate((keep_ref, swap_ref)):
        start = place[1 + n]
        at = pl.multiple_of(jnp.minimum(start // SEQ * SEQ, D - window), SEQ)
        turned_ref[...] = scaled(grad_ref[:, pl.ds(at, window)]).astype(jnp.float32).T
        inside = pl.multiple_of(start - at, 16)
        piece_ref[...] = turned_ref[pl.ds(inside, ROWS), :].astype(jnp.bfloat16)


def partial_squares(place, seg_rows, counts, hidden, grad_out):
    vmem, smem = pl.BlockSpec(memory_space=pltpu.VMEM), pl.BlockSpec(memory_space=pltpu.SMEM)
    piece = jax.ShapeDtypeStruct((ROWS, SEQ), jnp.bfloat16)
    return pl.pallas_call(
        squares_kernel,
        in_specs=[smem, vmem, smem, vmem, vmem],
        out_specs=[vmem] * 3,
        out_shape=[jax.ShapeDtypeStruct((2 * NSEG, SEQ), jnp.float32), piece, piece],
        scratch_shapes=[pltpu.VMEM((3 * SEQ, SEQ), jnp.float32)],
        compiler_params=pltpu.CompilerParams(vmem_limit_bytes=56 * 1024 * 1024),
    )(place, seg_rows, counts, hidden, grad_out)


def order_kernel(place, *refs):
    quarters, out_refs = refs[:ROW], refs[ROW:]
    for b in range(2):
        for i in range(PLANES):
            for k in range(ROW):

                @pl.when(place[0, b * PLANES + i] == k)
                def _(b=b, i=i, k=k):
                    out_refs[b][:, i * SEQ : (i + 1) * SEQ] = quarters[k][place[1, b * PLANES + i]]


def in_order(place, quarters):
    vmem = pl.BlockSpec(memory_space=pltpu.VMEM)
    return pl.pallas_call(
        order_kernel,
        in_specs=[pl.BlockSpec(memory_space=pltpu.SMEM)] + [vmem] * ROW,
        out_specs=[vmem, vmem],
        out_shape=[jax.ShapeDtypeStruct((ROWS, PLANES * SEQ), jnp.bfloat16)] * 2,
        compiler_params=pltpu.CompilerParams(vmem_limit_bytes=24 * 1024 * 1024),
    )(place, *quarters)


def product_kernel(*refs):
    w_ref, h_ref, *noise_ref = refs[:-1]
    summed = jnp.dot(w_ref[...], h_ref[...], preferred_element_type=jnp.float32)
    for ref in noise_ref:
        summed += ref[...].astype(jnp.float32)
    refs[-1][...] = summed.astype(refs[-1].dtype)


def product(rows, h_all, *noise):
    tokens, columns = h_all.shape
    vmem = pl.BlockSpec(memory_space=pltpu.VMEM)
    return pl.pallas_call(
        product_kernel,
        in_specs=[vmem] * (2 + len(noise)),
        out_specs=vmem,
        out_shape=jax.ShapeDtypeStruct((ROWS, columns), jnp.float32 if noise else jnp.bfloat16),
        compiler_params=pltpu.CompilerParams(vmem_limit_bytes=24 * 1024 * 1024),
        cost_estimate=pl.CostEstimate(
            flops=2 * tokens * ROWS * columns, bytes_accessed=2 * tokens * (ROWS + columns), transcendentals=0
        ),
    )(rows, h_all, *noise)


def per_device(hidden, grad_out, seg_ids, seg_counts, added_noise):
    pair, parity, core = lax.axis_index("pair"), lax.axis_index("parity"), lax.axis_index("core")
    x, y = lax.axis_index("x"), lax.axis_index("y")
    plane, j = pair * 2 + parity, y * ROW + x
    dp = plane * 2 + core
    h_all = lax.all_gather(hidden, ("pair", "core"), axis=0, tiled=True)

    seg_rows = seg_ids.reshape(-1, SEQ)

    def start(to_plane, of_core):
        shift = jnp.where(y < 2, 0, 1 - 2 * of_core)
        return ((to_plane + shift + PLANES) % PLANES * 2 + of_core) * ROWS

    ahead = plane + 2 * (j % PAIRS)
    here = jnp.stack([dp, start(ahead, core), start(ahead + 8, 1 - core)]).astype(jnp.int32)
    squares, keep, swap = partial_squares(here, seg_rows, seg_counts, hidden, grad_out)
    squares = lax.psum(lax.psum(squares, "x"), "y")
    norms = jnp.sqrt(squares[:NSEG, 0] + EPSILON)
    factor = jnp.minimum(1.0, clip_bound() / jnp.sqrt(squares[NSEG : NSEG + 1] + EPSILON))

    def weighted(scaled):
        return (scaled.astype(jnp.float32) * factor).astype(jnp.bfloat16)

    keep, swap = fan_out(weighted(keep), 0, False), fan_out(weighted(swap), 4, True)
    row = lax.all_gather(jnp.stack([keep, swap]), "x", axis=0, tiled=True)
    one, two, three = [along_y(row, k) for k in range(1, ROW)]
    quarters = [row, one, two, three]

    sequence = jnp.arange(PLANES)
    other = (sequence % 2 != core).astype(jnp.int32)
    came = (pair - sequence // 2 + 2 * PAIRS - 4 * other) % PAIRS
    inside = came % ROW * 2 + other

    quarter = jnp.concatenate([came // ROW, 2 + came // ROW]) ^ y
    place = jnp.stack([quarter, jnp.tile(inside, 2)]).astype(jnp.int32)
    own, neighbours = in_order(place, quarters)
    own, neighbours, h_all = lax.optimization_barrier((own, neighbours, h_all))
    handed = to_neighbour(product(neighbours, h_all))
    summed = product(own, h_all, added_noise)
    weight_grad = (summed + handed.astype(jnp.float32)).astype(jnp.bfloat16)
    return (weight_grad, norms)


def solution(mesh):
    split = Mesh(mesh.devices.reshape(PAIRS, 2, 2, ROW, ROW), ("pair", "parity", "core", "y", "x"))
    dp, tensor = ("pair", "parity", "core"), ("y", "x")
    placed = (P(dp, tensor), P(dp, None), P(), P(dp), P(dp, tensor))
    return jax.shard_map(
        per_device,
        mesh=split,
        in_specs=placed,
        out_specs=(P(dp, tensor), P(dp)),
        check_vma=False,
    )
```

```python
import jax
import jax.numpy as jnp
from jax import lax
from jax.experimental import pallas as pl
from jax.experimental.pallas import tpu as pltpu
from jax.sharding import Mesh
from jax.sharding import PartitionSpec as P

D = 4608
FFW = 18432
SEQ = 128
NSEG = 8
PLANES = 16
PAIRS = PLANES // 2
ROW = 4
ROWS = 144

EPSILON = 1e-06
CLIP_FRACTION = 4.2


def clip_bound():
    return CLIP_FRACTION * (FFW * D * NSEG / SEQ) ** 0.5


def along_y(value, distance):
    return lax.ppermute(value, "y", [(i, i ^ distance) for i in range(ROW)])


def fan_out(value, extra, cross):
    perm = []
    for plane in range(PLANES):
        for core in range(2):
            for j in range(ROW * ROW):
                to = ((plane + 2 * (j % PAIRS + extra)) % PLANES) * 2 + (1 - core if cross else core)
                perm.append(((plane * 2 + core) * 16 + j, to * 16 + j))
    return lax.ppermute(value, ("pair", "parity", "core", "y", "x"), perm)


def to_neighbour(value):
    perm = [(plane * 2 + core, (plane + 1 - 2 * core) % PLANES * 2 + core) for plane in range(PLANES) for core in range(2)]
    return lax.ppermute(value, ("pair", "parity", "core"), perm)


def block_starts():
    plane, core = lax.axis_index("pair") * 2 + lax.axis_index("parity"), lax.axis_index("core")
    x, y = lax.axis_index("x"), lax.axis_index("y")
    ahead = plane + 2 * ((y * ROW + x) % PAIRS)

    def start(to_plane, of_core):
        shift = jnp.where(y < 2, 0, 1 - 2 * of_core)
        return ((to_plane + shift + PLANES) % PLANES * 2 + of_core) * ROWS

    return plane * 2 + core, (start(ahead, core), start(ahead + 8, 1 - core))


def squares_kernel(seg_ref, count_ref, hidden_ref, grad_ref, out_ref, keep_ref, swap_ref, turned_ref):
    dp, starts = block_starts()
    seg = seg_ref[pl.ds(dp, 1), :]
    row = lax.broadcasted_iota(jnp.int32, (SEQ, SEQ), 0)
    column = lax.broadcasted_iota(jnp.int32, (SEQ, SEQ), 1)
    count = jnp.zeros((1, SEQ), jnp.float32)
    for i in range(NSEG):
        count = jnp.where(seg == i, count_ref[i].astype(jnp.float32), count)
    count_column = jnp.sum(jnp.where(row == column, count, 0.0), axis=1, keepdims=True)

    def scaled(block):
        return (block.astype(jnp.float32) / count_column).astype(jnp.bfloat16)

    contract = (((1,), (1,)), ((), ()))
    gram_hidden = lax.dot_general(
        hidden_ref[...], hidden_ref[...], contract, preferred_element_type=jnp.float32
    )
    gram_scaled = jnp.zeros((SEQ, SEQ), jnp.float32)
    width = 512
    for k in range(D // width):
        block = scaled(grad_ref[:, k * width : (k + 1) * width])
        gram_scaled += lax.dot_general(block, block, contract, preferred_element_type=jnp.float32)
    seg_wide = seg.astype(jnp.float32)
    seg_column = jnp.sum(jnp.where(row == column, seg_wide, 0.0), axis=1, keepdims=True)
    products = jnp.where(seg_column == seg_wide, gram_hidden * gram_scaled, 0.0)
    columns = jnp.sum(products, axis=0, keepdims=True)
    example = lax.broadcasted_iota(jnp.int32, (NSEG, SEQ), 0)
    total = jnp.sum(jnp.where(example == seg, columns, 0.0), axis=1, keepdims=True)
    of_token = jnp.sum(jnp.where(example == seg, total, 0.0), axis=0, keepdims=True)
    out_ref[:NSEG, :] = jnp.broadcast_to(total, (NSEG, SEQ))
    out_ref[NSEG:, :] = jnp.broadcast_to(of_token, (NSEG, SEQ))

    window = turned_ref.shape[0]
    for n, piece_ref in enumerate((keep_ref, swap_ref)):
        start = starts[n]
        at = pl.multiple_of(jnp.minimum(start // SEQ * SEQ, D - window), SEQ)
        turned_ref[...] = scaled(grad_ref[:, pl.ds(at, window)]).astype(jnp.float32).T
        inside = pl.multiple_of(start - at, 16)
        piece_ref[...] = turned_ref[pl.ds(inside, ROWS), :].astype(jnp.bfloat16)


def partial_squares(seg_rows, counts, hidden, grad_out):
    vmem, smem = pl.BlockSpec(memory_space=pltpu.VMEM), pl.BlockSpec(memory_space=pltpu.SMEM)
    piece = jax.ShapeDtypeStruct((ROWS, SEQ), jnp.bfloat16)
    return pl.pallas_call(
        squares_kernel,
        in_specs=[vmem, smem, vmem, vmem],
        out_specs=[vmem] * 3,
        out_shape=[jax.ShapeDtypeStruct((2 * NSEG, SEQ), jnp.float32), piece, piece],
        scratch_shapes=[pltpu.VMEM((3 * SEQ, SEQ), jnp.float32)],
        compiler_params=pltpu.CompilerParams(vmem_limit_bytes=56 * 1024 * 1024),
    )(seg_rows, counts, hidden, grad_out)


def order_kernel(place, *refs):
    quarters, out_refs = refs[:ROW], refs[ROW:]
    for b in range(2):
        for i in range(PLANES):
            for k in range(ROW):

                @pl.when(place[0, b * PLANES + i] == k)
                def _(b=b, i=i, k=k):
                    out_refs[b][:, i * SEQ : (i + 1) * SEQ] = quarters[k][place[1, b * PLANES + i]]


def in_order(place, quarters):
    vmem = pl.BlockSpec(memory_space=pltpu.VMEM)
    return pl.pallas_call(
        order_kernel,
        in_specs=[pl.BlockSpec(memory_space=pltpu.SMEM)] + [vmem] * ROW,
        out_specs=[vmem, vmem],
        out_shape=[jax.ShapeDtypeStruct((ROWS, PLANES * SEQ), jnp.bfloat16)] * 2,
        compiler_params=pltpu.CompilerParams(vmem_limit_bytes=24 * 1024 * 1024),
    )(place, *quarters)


def product_kernel(*refs):
    w_ref, h_ref, *noise_ref = refs[:-1]
    summed = jnp.dot(w_ref[...], h_ref[...], preferred_element_type=jnp.float32)
    for ref in noise_ref:
        summed += ref[...].astype(jnp.float32)
    refs[-1][...] = summed.astype(refs[-1].dtype)


def product(rows, h_all, *noise):
    tokens, columns = h_all.shape
    vmem = pl.BlockSpec(memory_space=pltpu.VMEM)
    return pl.pallas_call(
        product_kernel,
        in_specs=[vmem] * (2 + len(noise)),
        out_specs=vmem,
        out_shape=jax.ShapeDtypeStruct((ROWS, columns), jnp.float32 if noise else jnp.bfloat16),
        compiler_params=pltpu.CompilerParams(vmem_limit_bytes=24 * 1024 * 1024),
        cost_estimate=pl.CostEstimate(
            flops=2 * tokens * ROWS * columns, bytes_accessed=2 * tokens * (ROWS + columns), transcendentals=0
        ),
    )(rows, h_all, *noise)


def per_device(hidden, grad_out, seg_ids, seg_counts, added_noise):
    pair, parity, core = lax.axis_index("pair"), lax.axis_index("parity"), lax.axis_index("core")
    x, y = lax.axis_index("x"), lax.axis_index("y")
    plane, j = pair * 2 + parity, y * ROW + x
    dp = plane * 2 + core
    h_all = lax.all_gather(hidden, ("pair", "core"), axis=0, tiled=True)

    seg_rows = seg_ids.reshape(-1, SEQ)

    squares, keep, swap = partial_squares(seg_rows, seg_counts, hidden, grad_out)
    squares = lax.psum(lax.psum(squares, "x"), "y")
    norms = jnp.sqrt(squares[:NSEG, 0] + EPSILON)
    factor = jnp.minimum(1.0, clip_bound() / jnp.sqrt(squares[NSEG : NSEG + 1] + EPSILON))

    def weighted(scaled):
        return (scaled.astype(jnp.float32) * factor).astype(jnp.bfloat16)

    keep, swap = fan_out(weighted(keep), 0, False), fan_out(weighted(swap), 4, True)
    row = lax.all_gather(jnp.stack([keep, swap]), "x", axis=0, tiled=True)
    one, two, three = [along_y(row, k) for k in range(1, ROW)]
    quarters = [row, one, two, three]

    sequence = jnp.arange(PLANES)
    other = (sequence % 2 != core).astype(jnp.int32)
    came = (pair - sequence // 2 + 2 * PAIRS - 4 * other) % PAIRS
    inside = came % ROW * 2 + other

    quarter = jnp.concatenate([came // ROW, 2 + came // ROW]) ^ y
    place = jnp.stack([quarter, jnp.tile(inside, 2)]).astype(jnp.int32)
    own, neighbours = in_order(place, quarters)
    own, neighbours, h_all = lax.optimization_barrier((own, neighbours, h_all))
    handed = to_neighbour(product(neighbours, h_all))
    summed = product(own, h_all, added_noise)
    weight_grad = (summed + handed.astype(jnp.float32)).astype(jnp.bfloat16)
    return (weight_grad, norms)


def solution(mesh):
    split = Mesh(mesh.devices.reshape(PAIRS, 2, 2, ROW, ROW), ("pair", "parity", "core", "y", "x"))
    dp, tensor = ("pair", "parity", "core"), ("y", "x")
    placed = (P(dp, tensor), P(dp, None), P(), P(dp), P(dp, tensor))
    return jax.shard_map(
        per_device,
        mesh=split,
        in_specs=placed,
        out_specs=(P(dp, tensor), P(dp)),
        check_vma=False,
    )
```

```python
import jax
import jax.numpy as jnp
from jax import lax
from jax.experimental import pallas as pl
from jax.experimental.pallas import tpu as pltpu
from jax.sharding import Mesh
from jax.sharding import PartitionSpec as P

D = 4608
FFW = 18432
SEQ = 128
NSEG = 8
PLANES = 16
PAIRS = PLANES // 2
ROW = 4
ROWS = 144

EPSILON = 1e-06
CLIP_FRACTION = 4.2


def clip_bound():
    return CLIP_FRACTION * (FFW * D * NSEG / SEQ) ** 0.5


def along_y(value, distance):
    return lax.ppermute(value, "y", [(i, i ^ distance) for i in range(ROW)])


def fan_out(value, extra, cross):
    perm = []
    for plane in range(PLANES):
        for core in range(2):
            for j in range(ROW * ROW):
                to = ((plane + 2 * (j % PAIRS + extra)) % PLANES) * 2 + (1 - core if cross else core)
                perm.append(((plane * 2 + core) * 16 + j, to * 16 + j))
    return lax.ppermute(value, ("pair", "parity", "core", "y", "x"), perm)


def to_neighbour(value):
    perm = [(plane * 2 + core, (plane + 1 - 2 * core) % PLANES * 2 + core) for plane in range(PLANES) for core in range(2)]
    return lax.ppermute(value, ("pair", "parity", "core"), perm)


def block_starts():
    plane, core = lax.axis_index("pair") * 2 + lax.axis_index("parity"), lax.axis_index("core")
    x, y = lax.axis_index("x"), lax.axis_index("y")
    ahead = plane + 2 * ((y * ROW + x) % PAIRS)

    def start(to_plane, of_core):
        shift = jnp.where(y < 2, 0, 1 - 2 * of_core)
        return ((to_plane + shift + PLANES) % PLANES * 2 + of_core) * ROWS

    return plane * 2 + core, (start(ahead, core), start(ahead + 8, 1 - core))


def squares_kernel(seg_ref, count_ref, hidden_ref, grad_ref, out_ref, keep_ref, swap_ref, turned_ref):
    dp, starts = block_starts()
    seg = seg_ref[pl.ds(dp, 1), :]
    row = lax.broadcasted_iota(jnp.int32, (SEQ, SEQ), 0)
    column = lax.broadcasted_iota(jnp.int32, (SEQ, SEQ), 1)
    count = jnp.zeros((1, SEQ), jnp.float32)
    for i in range(NSEG):
        count = jnp.where(seg == i, count_ref[i].astype(jnp.float32), count)
    count_column = jnp.sum(jnp.where(row == column, count, 0.0), axis=1, keepdims=True)

    def scaled(block):
        return (block.astype(jnp.float32) / count_column).astype(jnp.bfloat16)

    contract = (((1,), (1,)), ((), ()))
    gram_hidden = lax.dot_general(
        hidden_ref[...], hidden_ref[...], contract, preferred_element_type=jnp.float32
    )
    gram_scaled = jnp.zeros((SEQ, SEQ), jnp.float32)
    width = 1152
    for k in range(D // width):
        block = scaled(grad_ref[:, k * width : (k + 1) * width])
        gram_scaled += lax.dot_general(block, block, contract, preferred_element_type=jnp.float32)
    seg_wide = seg.astype(jnp.float32)
    seg_column = jnp.sum(jnp.where(row == column, seg_wide, 0.0), axis=1, keepdims=True)
    products = jnp.where(seg_column == seg_wide, gram_hidden * gram_scaled, 0.0)
    columns = jnp.sum(products, axis=0, keepdims=True)
    example = lax.broadcasted_iota(jnp.int32, (NSEG, SEQ), 0)
    total = jnp.sum(jnp.where(example == seg, columns, 0.0), axis=1, keepdims=True)
    of_token = jnp.sum(jnp.where(example == seg, total, 0.0), axis=0, keepdims=True)
    out_ref[:NSEG, :] = jnp.broadcast_to(total, (NSEG, SEQ))
    out_ref[NSEG:, :] = jnp.broadcast_to(of_token, (NSEG, SEQ))

    window = turned_ref.shape[0]
    for n, piece_ref in enumerate((keep_ref, swap_ref)):
        start = starts[n]
        at = pl.multiple_of(jnp.minimum(start // SEQ * SEQ, D - window), SEQ)
        turned_ref[...] = scaled(grad_ref[:, pl.ds(at, window)]).astype(jnp.float32).T
        inside = pl.multiple_of(start - at, 16)
        piece_ref[...] = turned_ref[pl.ds(inside, ROWS), :].astype(jnp.bfloat16)


def partial_squares(seg_rows, counts, hidden, grad_out):
    vmem, smem = pl.BlockSpec(memory_space=pltpu.VMEM), pl.BlockSpec(memory_space=pltpu.SMEM)
    piece = jax.ShapeDtypeStruct((ROWS, SEQ), jnp.bfloat16)
    return pl.pallas_call(
        squares_kernel,
        in_specs=[vmem, smem, vmem, vmem],
        out_specs=[vmem] * 3,
        out_shape=[jax.ShapeDtypeStruct((2 * NSEG, SEQ), jnp.float32), piece, piece],
        scratch_shapes=[pltpu.VMEM((3 * SEQ, SEQ), jnp.float32)],
        compiler_params=pltpu.CompilerParams(vmem_limit_bytes=56 * 1024 * 1024),
    )(seg_rows, counts, hidden, grad_out)


def order_kernel(place, *refs):
    quarters, out_refs = refs[:ROW], refs[ROW:]
    for b in range(2):
        for i in range(PLANES):
            for k in range(ROW):

                @pl.when(place[0, b * PLANES + i] == k)
                def _(b=b, i=i, k=k):
                    out_refs[b][:, i * SEQ : (i + 1) * SEQ] = quarters[k][place[1, b * PLANES + i]]


def in_order(place, quarters):
    vmem = pl.BlockSpec(memory_space=pltpu.VMEM)
    return pl.pallas_call(
        order_kernel,
        in_specs=[pl.BlockSpec(memory_space=pltpu.SMEM)] + [vmem] * ROW,
        out_specs=[vmem, vmem],
        out_shape=[jax.ShapeDtypeStruct((ROWS, PLANES * SEQ), jnp.bfloat16)] * 2,
        compiler_params=pltpu.CompilerParams(vmem_limit_bytes=24 * 1024 * 1024),
    )(place, *quarters)


def product_kernel(*refs):
    w_ref, h_ref, *noise_ref = refs[:-1]
    summed = jnp.dot(w_ref[...], h_ref[...], preferred_element_type=jnp.float32)
    for ref in noise_ref:
        summed += ref[...].astype(jnp.float32)
    refs[-1][...] = summed.astype(refs[-1].dtype)


def product(rows, h_all, *noise):
    tokens, columns = h_all.shape
    vmem = pl.BlockSpec(memory_space=pltpu.VMEM)
    return pl.pallas_call(
        product_kernel,
        in_specs=[vmem] * (2 + len(noise)),
        out_specs=vmem,
        out_shape=jax.ShapeDtypeStruct((ROWS, columns), jnp.float32 if noise else jnp.bfloat16),
        compiler_params=pltpu.CompilerParams(vmem_limit_bytes=24 * 1024 * 1024),
        cost_estimate=pl.CostEstimate(
            flops=2 * tokens * ROWS * columns, bytes_accessed=2 * tokens * (ROWS + columns), transcendentals=0
        ),
    )(rows, h_all, *noise)


def per_device(hidden, grad_out, seg_ids, seg_counts, added_noise):
    pair, parity, core = lax.axis_index("pair"), lax.axis_index("parity"), lax.axis_index("core")
    x, y = lax.axis_index("x"), lax.axis_index("y")
    plane, j = pair * 2 + parity, y * ROW + x
    dp = plane * 2 + core
    h_all = lax.all_gather(hidden, ("pair", "core"), axis=0, tiled=True)

    seg_rows = seg_ids.reshape(-1, SEQ)

    squares, keep, swap = partial_squares(seg_rows, seg_counts, hidden, grad_out)
    squares = lax.psum(lax.psum(squares, "x"), "y")
    norms = jnp.sqrt(squares[:NSEG, 0] + EPSILON)
    factor = jnp.minimum(1.0, clip_bound() / jnp.sqrt(squares[NSEG : NSEG + 1] + EPSILON))

    def weighted(scaled):
        return (scaled.astype(jnp.float32) * factor).astype(jnp.bfloat16)

    keep, swap = fan_out(weighted(keep), 0, False), fan_out(weighted(swap), 4, True)
    row = lax.all_gather(jnp.stack([keep, swap]), "x", axis=0, tiled=True)
    one, two, three = [along_y(row, k) for k in range(1, ROW)]
    quarters = [row, one, two, three]

    sequence = jnp.arange(PLANES)
    other = (sequence % 2 != core).astype(jnp.int32)
    came = (pair - sequence // 2 + 2 * PAIRS - 4 * other) % PAIRS
    inside = came % ROW * 2 + other

    quarter = jnp.concatenate([came // ROW, 2 + came // ROW]) ^ y
    place = jnp.stack([quarter, jnp.tile(inside, 2)]).astype(jnp.int32)
    own, neighbours = in_order(place, quarters)
    own, neighbours, h_all = lax.optimization_barrier((own, neighbours, h_all))
    handed = to_neighbour(product(neighbours, h_all))
    summed = product(own, h_all, added_noise)
    weight_grad = (summed + handed.astype(jnp.float32)).astype(jnp.bfloat16)
    return (weight_grad, norms)


def solution(mesh):
    split = Mesh(mesh.devices.reshape(PAIRS, 2, 2, ROW, ROW), ("pair", "parity", "core", "y", "x"))
    dp, tensor = ("pair", "parity", "core"), ("y", "x")
    placed = (P(dp, tensor), P(dp, None), P(), P(dp), P(dp, tensor))
    return jax.shard_map(
        per_device,
        mesh=split,
        in_specs=placed,
        out_specs=(P(dp, tensor), P(dp)),
        check_vma=False,
    )
```
